128 devices in a mesh: gx: 16 (over z, x_hi, core), gy: 8 (over x_lo, y).
Axes of the slice: x: 4 (x_hi: 2, x_lo: 2; x = x_hi * 2 + x_lo), y: 4, z: 4, core: 2. Of those that a mesh axis runs over, the one named last changes fastest.
Arguments:
- heights: bfloat16 [4, 1024, 4096], P(None, 'gx', 'gy'), may hold values from -6 to 6
- probes: float32 [4, 1024, 4096], P(None, 'gx', 'gy'), may hold values from -6 to 6
- cotangent: float32 [1024, 4096], P('gx', 'gy'), may hold values from -6 to 6
Outputs:
- hessian_probes: float32 [4, 1024, 4096], P(None, 'gx', 'gy')
- gradient: float32 [1024, 4096], P('gx', 'gy')
The draws below stay inside these ranges and needn't reach their ends.
All inputs are finite; a program needn't handle non-finite values.
Results may differ from the reference program's by a relative error of at most 0.0003.
Values sent between devices are 32-bit elements; how exact they have to be, the bound alone decides.
A program may use at most 64 MiB of HBM per device.

```python
import jax
import jax.numpy as jnp

STEPS = 4
PROBES = 4
NX = 1024
NY = 4096


def block_scale(stream_key, dims, pieces, least, top_value):
    factor_of = 1.0
    for dim, parts in pieces:
        steps = jax.random.uniform(jax.random.fold_in(jax.random.fold_in(stream_key, 6), dim), (parts,), jnp.float32, least / len(pieces), top_value / len(pieces))
        factor_of = factor_of * jnp.repeat(jnp.exp(steps), dims[dim] // parts).reshape((-1,) + (1,) * (len(dims) - 1 - dim))
    return factor_of


def noise(stream_key, extent, width, reach, cuts=(), dtype=jnp.bfloat16):
    array = width * jax.random.normal(stream_key, extent, jnp.float32)
    if cuts:
        array = array * block_scale(stream_key, extent, cuts, -0.22, 0.18)
    return jnp.clip(array, -reach, reach).astype(dtype)


def setup_inputs(seed: int = 0) -> dict:
    splits = jax.random.split(jax.random.key(seed), 4)
    return {
        "heights": noise(splits[0], (STEPS, NX, NY), 1.0, 6.0, ((1, 16), (2, 8))),
        "probes": noise(splits[1], (PROBES, NX, NY), 1.0, 6.0, ((1, 16), (2, 8)), jnp.float32),
        "cotangent": noise(splits[2], (NX, NY), 1.0, 6.0, ((0, 16), (1, 8)), jnp.float32),
    }


time_step = 0.05
viscosity = 3.0
coupling = 3.0


def derivative(source, dimension):
    return (jnp.roll(source, 2, dimension) - 8.0 * jnp.roll(source, 1, dimension) + 8.0 * jnp.roll(source, -1, dimension) - jnp.roll(source, -2, dimension)) / 12.0


def curvature(source, dimension):
    return (-jnp.roll(source, 2, dimension) + 16.0 * jnp.roll(source, 1, dimension) - 30.0 * source + 16.0 * jnp.roll(source, -1, dimension) - jnp.roll(source, -2, dimension)) / 12.0


def laplacian(source):
    return curvature(source, -2) + curvature(source, -1)


def reference(heights, probes, cotangent):
    tangent = probes.astype(jnp.float32)
    tangents = []
    for counter in range(STEPS):
        height = heights[counter].astype(jnp.float32)
        along_x = derivative(height, -2)
        along_y = derivative(height, -1)
        tangents.append(tangent)
        if counter + 1 < STEPS:
            tangent_x = derivative(tangent, -2)
            tangent_y = derivative(tangent, -1)
            tangent = tangent + time_step * (viscosity * laplacian(tangent) + coupling * (along_x * tangent_x + along_y * tangent_y))
    adjoint = cotangent.astype(jnp.float32)
    second = jnp.zeros(probes.shape, jnp.float32)
    for counter in reversed(range(STEPS)):
        height = heights[counter].astype(jnp.float32)
        along_x = derivative(height, -2)
        along_y = derivative(height, -1)
        tangent = tangents[counter]
        tangent_x = derivative(tangent, -2)
        tangent_y = derivative(tangent, -1)
        flux_x = adjoint * along_x
        flux_y = adjoint * along_y
        mixed_x = second * along_x + adjoint * tangent_x
        mixed_y = second * along_y + adjoint * tangent_y
        new_adjoint = adjoint + time_step * (viscosity * laplacian(adjoint) - coupling * (derivative(flux_x, -2) + derivative(flux_y, -1)))
        second = second + time_step * (viscosity * laplacian(second) - coupling * (derivative(mixed_x, -2) + derivative(mixed_y, -1)))
        adjoint = new_adjoint
    return second, adjoint
```

```python
import functools

import jax
import jax.numpy as jnp
from jax import lax
from jax.experimental import pallas as pl
from jax.experimental.pallas import tpu as pltpu
from jax.sharding import PartitionSpec as P

STEPS = 4
PROBES = 4
TILES = 5
REACH = 16
ROWS, COLS = 64, 512
SPAN = ROWS + 2 * REACH

time_step = 0.05
viscosity = 3.0
coupling = 3.0
A = time_step * viscosity / 12.0
KEEP = 1.0 - 60.0 * A
SLOPE = 1.0 / 12.0

WIDTHS = [16] * PROBES + [16, 14, 12, 10] + [8]
LANES = [sum(WIDTHS[:f]) for f in range(len(WIDTHS))]
PACK_ROWS = [0, 16, 30, 42, 52]
MESH = pl.DeviceIdType.MESH


def left(x, by):
    return pltpu.roll(x, by % 128, 1)


def lanes(rows):
    return lax.broadcasted_iota(jnp.int32, (rows, 128), 1)


def kernel(
    heights, probes, cotangent, q_out, p_out,
    hb, ub, cb, send_rows, rows_u, rows_h, send_cols, cols,
    H, U0, U1, U2, U3, AR, AC, BR, BC, PP, MP, M3, N3, Q3, Q2, QR, Q1, M2, M1, M0,
    local_sem, send_sem, recv_sem, far_sem,
):
    gx, gy = lax.axis_index("gx"), lax.axis_index("gy")
    n_gx, n_gy = lax.axis_size("gx"), lax.axis_size("gy")
    core = lax.rem(gx, 2)
    late = lax.rem(lax.div(gx, 2), 2)
    near_gx = gx + 1 - 2 * core
    far_gx = lax.rem(gx - 1 + 2 * core + n_gx, n_gx)
    west, east = lax.rem(gy + n_gy - 1, n_gy), lax.rem(gy + 1, n_gy)
    near_group = [(near_gx, gy), (gx, west), (gx, east), (near_gx, west), (near_gx, east)]
    far_group = [(far_gx, gy), (far_gx, west), (far_gx, east)]

    loads = [
        pltpu.make_async_copy(heights, hb, local_sem.at[0]),
        pltpu.make_async_copy(cotangent, cb, local_sem.at[1]),
        pltpu.make_async_copy(probes, ub, local_sem.at[2]),
    ]
    for c in loads:
        c.start()

    barrier = pltpu.get_barrier_semaphore()
    for d in near_group:
        pl.semaphore_signal(barrier, inc=1, device_id=d, device_id_type=MESH)

    near_edge, far_edge = 1 - core, core
    near_halo, far_halo = 1 - core, core

    def copy(src, dst, s, d):
        return pltpu.make_async_remote_copy(
            src_ref=src, dst_ref=dst, send_sem=send_sem.at[s], recv_sem=recv_sem.at[s],
            device_id=d, device_id_type=MESH,
        )

    def row_start(edge):
        return pl.multiple_of(edge * (ROWS - REACH), 16)

    def halo_start(halo):
        return pl.multiple_of(halo * (SPAN - REACH), 16)

    def u_copy(edge, p, s, d):
        return copy(probes.at[p, pl.ds(row_start(edge), REACH)], rows_u.at[1 - edge, p], s, d)

    def h_copy(edge, s, d):
        part = (slice(None), pl.ds(0, 64))
        return copy(send_rows.at[(edge, *part)], rows_h.at[(1 - edge, *part)], s, d)

    def c_copy(side, s, d):
        return copy(send_cols.at[side], cols.at[1 - side, pl.ds(REACH, ROWS)], s, d)

    def k_copy(side, edge, s, d):
        return copy(
            send_cols.at[side, pl.ds(row_start(edge), REACH)],
            cols.at[1 - side, pl.ds(halo_start(1 - edge), REACH)], s, d,
        )

    far_u = [u_copy(far_edge, p, p, far_group[0]) for p in range(PROBES)]
    far_h = h_copy(far_edge, 4, far_group[0])
    far_k = [k_copy(0, far_edge, 5, far_group[1]), k_copy(1, far_edge, 6, far_group[2])]
    near_u = [u_copy(near_edge, p, 7 + p, near_group[0]) for p in range(PROBES)]
    near_h = h_copy(near_edge, 11, near_group[0])
    near_k = [k_copy(0, near_edge, 12, near_group[3]), k_copy(1, near_edge, 13, near_group[4])]
    side_c = [c_copy(0, 14, near_group[1]), c_copy(1, 15, near_group[2])]

    @pl.when(late == 0)
    def _():
        pl.semaphore_wait(barrier, 5)
        for d in far_group:
            pl.semaphore_signal(barrier, inc=1, device_id=d, device_id_type=MESH)

    @pl.when(late == 1)
    def _():
        pl.semaphore_wait(barrier, 8)
        for c in far_u:
            c.start()
        for d in far_group:
            pl.semaphore_signal(far_sem, inc=1, device_id=d, device_id_type=MESH)

    for c in near_u:
        c.start()

    loads[0].wait()
    loads[1].wait()
    for n in range(4):
        cut = slice(128 * n, 128 * n + 128)
        for k in range(STEPS):
            send_rows[0, n, PACK_ROWS[k] : PACK_ROWS[k] + 16] = hb[k, 0:16, cut].astype(jnp.float32)
        send_rows[0, n, 52:60] = cb[0:8, cut]
        for k in reversed(range(STEPS)):
            first = PACK_ROWS[k] - 2 * k
            send_rows[1, n, first : first + 16] = hb[k, 48:64, cut].astype(jnp.float32)
        send_rows[1, n, 52:60] = cb[56:64, cut]
    near_h.start()

    @pl.when(late == 1)
    def _():
        far_h.start()

    loads[2].wait()
    lane = lanes(ROWS)
    for side in (0, 1):
        packed = None
        for f, (w, o) in enumerate(zip(WIDTHS, LANES)):
            cut = slice(0, 128) if side == 0 else slice(COLS - 128, COLS)
            if f < 4:
                x = ub[f, :, cut]
            elif f < 8:
                x = hb[f - 4, :, cut].astype(jnp.float32)
            else:
                x = cb[:, cut]
            x = left(x, o if side == 0 else o + w)
            packed = x if packed is None else jnp.where(lane < o, packed, x)
        send_cols[side] = packed
    for c in side_c + near_k:
        c.start()

    @pl.when(late == 1)
    def _():
        for c in far_k:
            c.start()

    def to_tiles(store, nat, before, after, f, rows):
        lane = lanes(rows)
        w, o = WIDTHS[f], LANES[f]
        store(0, jnp.where(lane < 16, left(before, 16 - w - o), left(nat[0], 16)))
        for j, (shift) in ((1, 40), (2, 64), (3, 88)):
            store(j, jnp.where(lane < shift, left(nat[j - 1], shift), left(nat[j], shift)))
        store(4, jnp.where(lane < 112, left(nat[3], 112), left(after, 112 - o)))

    def put(ref, lead, start, rows):
        def store(j, value):
            ref[(*lead, j, pl.ds(start, rows))] = value

        return store

    def load_own():
        before, after = cols[0, REACH : REACH + ROWS], cols[1, REACH : REACH + ROWS]
        for f in range(9):
            if f < 4:
                nat, dst = [ub[f, :, 128 * n : 128 * n + 128] for n in range(4)], put(U0, (f,), REACH, ROWS)
            elif f < 8:
                nat = [hb[f - 4, :, 128 * n : 128 * n + 128].astype(jnp.float32) for n in range(4)]
                dst = put(H, (f - 4,), REACH, ROWS)
            else:
                nat, dst = [cb[:, 128 * n : 128 * n + 128] for n in range(4)], put(PP, (4,), REACH, ROWS)
            to_tiles(dst, nat, before, after, f, ROWS)

    def load_halo(halo, fields):
        start = halo_start(halo)
        before, after = cols[0, pl.ds(start, REACH)], cols[1, pl.ds(start, REACH)]
        for f in fields:
            if f < 4:
                nat = [rows_u[halo, f, :, 128 * n : 128 * n + 128] for n in range(4)]
                dst = put(U0, (f,), start, REACH)
            else:
                k = f - 4
                shift = 2 * k
                first = PACK_ROWS[k] - (1 - halo) * shift
                nat = [rows_h[halo, n, pl.ds(first, REACH)] for n in range(4)]
                dst = put(H, (k,), start, REACH) if f < 8 else put(PP, (4,), start, REACH)
            to_tiles(dst, nat, before, after, f, REACH)

    def slopes(region):
        def body(k, _):
            start, rows = region(k)
            for j in range(TILES):
                at = lambda d: H[k, j, pl.ds(start + d, rows)]
                x = at(0)
                AR[k, j, pl.ds(start, rows)] = SLOPE * (8.0 * (at(1) - at(-1)) - (at(2) - at(-2)))
                AC[k, j, pl.ds(start, rows)] = SLOPE * (
                    8.0 * (left(x, -1) - left(x, 1)) - (left(x, -2) - left(x, 2))
                )
            return 0

        lax.fori_loop(0, STEPS, body, 0)

    def over(first, last, batch, body):
        if last - first == batch:
            for i in range(batch):
                body(first + i)
            return

        def step(i, _):
            for b in range(batch):
                body(first + i * batch + b)
            return 0

        lax.fori_loop(0, (last - first) // batch, step, 0)

    def tangent(k, source, target, region):
        start, rows = region

        def body(p):
            for j in range(TILES):
                here = pl.ds(start, rows)
                at = lambda d: source[p, j, pl.ds(start + d, rows)]
                x, n1, s1, n2, s2 = at(0), at(-1), at(1), at(-2), at(2)
                w1, e1, w2, e2 = left(x, 1), left(x, -1), left(x, 2), left(x, -2)
                br = 8.0 * (s1 - n1) - (s2 - n2)
                bc = 8.0 * (e1 - w1) - (e2 - w2)
                if target is None:
                    adjoint = SLOPE * PP[STEPS, j, here]
                    M3[p, j, here] = adjoint * br
                    N3[p, j, here] = adjoint * bc
                    continue
                BR[k, p, j, here] = SLOPE * br
                BC[k, p, j, here] = SLOPE * bc
                lap = 16.0 * ((n1 + s1) + (w1 + e1)) - ((n2 + s2) + (w2 + e2))
                target[p, j, here] = KEEP * x + A * (
                    lap + AR[k, j, here] * br + AC[k, j, here] * bc
                )

        return body

    def spread(q_at, m_at, my):
        x = q_at(0)
        two = x + x
        ring = left(two + my, 1) + left(two - my, -1)
        s = q_at(-1) + q_at(1)
        ring = ring + ((s + s) + (m_at(-1) - m_at(1)))
        outer = left(x + my, 2) + left(x - my, -2)
        outer = outer + ((q_at(-2) + q_at(2)) + (m_at(-2) - m_at(2)))
        return KEEP * x + A * (8.0 * ring - outer)

    def p_flux(region):
        start, rows = region
        here = pl.ds(start, rows)
        for j in range(TILES):
            MP[STEPS, j, here] = PP[STEPS, j, here] * AR[STEPS - 1, j, here]

    def p_step(k, region):
        start, rows = region
        here = pl.ds(start, rows)
        results = []
        for j in range(TILES):
            q_at = lambda d: PP[k + 1, j, pl.ds(start + d, rows)]
            m_at = lambda d: MP[k + 1, j, pl.ds(start + d, rows)]
            out = spread(q_at, m_at, q_at(0) * AC[k, j, here])
            if k > 0:
                PP[k, j, here] = out
                MP[k, j, here] = out * AR[k - 1, j, here]
            results.append(out)
        if k == 0:
            to_natural(p_out, (), results, start, rows)

    def to_natural(ref, lead, tiles, start, rows):
        lane = lanes(rows)
        moved = [left(t, s) for t, s in zip(tiles, (112, 88, 64, 40, 16))]
        first = pl.multiple_of(start - REACH, 16)
        for n, edge in enumerate((100, 76, 52, 28)):
            ref[(*lead, pl.ds(first, rows), slice(128 * n, 128 * n + 128))] = jnp.where(
                lane < edge, moved[n], moved[n + 1]
            )

    def q_first(region):
        start, rows = region

        def body(p):
            here = pl.ds(start, rows)
            for j in range(TILES):
                m_at = lambda d: M3[p, j, pl.ds(start + d, rows)]
                my = N3[p, j, here]
                ring = (left(my, 1) - left(my, -1)) + (m_at(-1) - m_at(1))
                outer = (left(my, 2) - left(my, -2)) + (m_at(-2) - m_at(2))
                out = A * (8.0 * ring - outer)
                Q3[p, j, here] = out
                M2[p, j, here] = out * AR[2, j, here] + PP[3, j, here] * BR[2, p, j, here]

        return body

    def q_step(k, source, flux, target, next_flux, region):
        start, rows = region

        def body(p):
            here = pl.ds(start, rows)
            results = []
            for j in range(TILES):
                q_at = lambda d: source[p, j, pl.ds(start + d, rows)]
                m_at = lambda d: flux[p, j, pl.ds(start + d, rows)]
                my = q_at(0) * AC[k, j, here] + PP[k + 1, j, here] * BC[k, p, j, here]
                out = spread(q_at, m_at, my)
                if target is not None:
                    target[p, j, here] = out
                if next_flux is not None:
                    next_flux[p, j, here] = out * AR[k - 1, j, here] + PP[k, j, here] * BR[k - 1, p, j, here]
                results.append(out)
            if target is None:
                to_natural(q_out, (p,), results, start, rows)

        return body

    def refresh(region):
        start, rows = region

        def body(p):
            here = pl.ds(start, rows)
            lane = lanes(rows)
            for j in range(TILES):
                x = Q2[p, j, here]
                if j > 0:
                    x = jnp.where(lane < 12, left(Q2[p, j - 1, here], -104), x)
                if j < TILES - 1:
                    x = jnp.where(lane >= 116, left(Q2[p, j + 1, here], 104), x)
                QR[p, j, here] = x
                M1[p, j, here] = x * AR[1, j, here] + PP[2, j, here] * BR[1, p, j, here]

        return body

    def shared(region):
        slopes(lambda k: region(2, k))
        p_flux(region(8))
        for k in reversed(range(STEPS)):
            p_step(k, region(16 - 2 * k))

    def sweep(region, first, last, batch):
        run = functools.partial(over, first, last, batch)
        run(tangent(0, U0, U1, region(2)))
        run(tangent(1, U1, U2, region(4)))
        run(tangent(2, U2, U3, region(6)))
        run(tangent(3, U3, None, region(8)))
        run(q_first(region(10)))
        run(q_step(2, Q3, M2, Q2, None, region(12)))
        run(refresh(region(12)))
        run(q_step(1, QR, M1, Q1, M0, region(14)))
        run(q_step(0, Q1, M0, None, None, region(16)))

    def main_region(margin, k=None):
        rows = (80 - 2 * margin + 7) // 8 * 8
        if margin == 16:
            return pl.multiple_of(32 - 16 * core, 16), rows
        return (1 - core) * (SPAN - margin - rows) + core * margin, rows

    for c in near_u + [near_h] + near_k + side_c:
        c.wait_recv()
    load_own()
    load_halo(near_halo, range(9))

    @pl.when(late == 0)
    def _():
        pl.semaphore_wait(far_sem, 3)
        for c in far_u + [far_h] + far_k:
            c.start()

    shared(main_region)
    sweep(main_region, 0, PROBES, 2)

    def wedge_region(margin, k=None):
        if margin == 16:
            return pl.multiple_of(16 + 48 * core, 16), REACH
        m = margin if k is None else 2 * k + 2
        return (1 - core) * m + core * (80 - m), REACH

    far_h.wait_recv()
    for c in far_k:
        c.wait_recv()
    load_halo(far_halo, range(4, 9))
    shared(wedge_region)
    for first in (0, 2):
        for p in (first, first + 1):
            far_u[p].wait_recv()
        load_halo(far_halo, (first, first + 1))
        sweep(wedge_region, first, first + 2, 2)

    for c in far_u + [far_h] + far_k + near_u + [near_h] + near_k + side_c:
        c.wait_send()


def on_device(heights, probes, cotangent):
    f32 = jnp.float32
    probe = pltpu.VMEM((PROBES, TILES, SPAN, 128), f32)
    return pl.pallas_call(
        kernel,
        out_shape=[
            jax.ShapeDtypeStruct((PROBES, ROWS, COLS), f32),
            jax.ShapeDtypeStruct((ROWS, COLS), f32),
        ],
        in_specs=[pl.BlockSpec(memory_space=pl.ANY)] * 3,
        out_specs=[pl.BlockSpec(memory_space=pltpu.VMEM)] * 2,
        scratch_shapes=[
            pltpu.VMEM((STEPS, ROWS, COLS), jnp.bfloat16),
            pltpu.VMEM((PROBES, ROWS, COLS), f32),
            pltpu.VMEM((ROWS, COLS), f32),
            pltpu.VMEM((2, 4, 72, 128), f32),
            pltpu.VMEM((2, PROBES, REACH, COLS), f32),
            pltpu.VMEM((2, 4, 72, 128), f32),
            pltpu.VMEM((2, ROWS, 128), f32),
            pltpu.VMEM((2, SPAN, 128), f32),
            probe,
            probe, probe, probe, probe,
            probe, probe,
            pltpu.VMEM((3, PROBES, TILES, SPAN, 128), f32),
            pltpu.VMEM((3, PROBES, TILES, SPAN, 128), f32),
            pltpu.VMEM((STEPS + 1, TILES, SPAN, 128), f32),
            pltpu.VMEM((STEPS + 1, TILES, SPAN, 128), f32),
            probe, probe, probe, probe, probe, probe, probe, probe, probe,
            pltpu.SemaphoreType.DMA((3,)),
            pltpu.SemaphoreType.DMA((16,)),
            pltpu.SemaphoreType.DMA((16,)),
            pltpu.SemaphoreType.REGULAR,
        ],
        compiler_params=pltpu.CompilerParams(
            collective_id=0, has_side_effects=True, vmem_limit_bytes=56 * 2**20
        ),
    )(heights, probes, cotangent)


def solution(mesh):
    in_specs = (P(None, "gx", "gy"), P(None, "gx", "gy"), P("gx", "gy"))
    out_specs = (P(None, "gx", "gy"), P("gx", "gy"))
    return jax.shard_map(
        on_device, mesh=mesh, in_specs=in_specs, out_specs=out_specs, check_vma=False
    )
```

```python
import functools

import jax
import jax.numpy as jnp
from jax import lax
from jax.experimental import pallas as pl
from jax.experimental.pallas import tpu as pltpu
from jax.sharding import PartitionSpec as P

STEPS = 4
PROBES = 4
TILES = 5
REACH = 16
ROWS, COLS = 64, 512
SPAN = ROWS + 2 * REACH

time_step = 0.05
viscosity = 3.0
coupling = 3.0
A = time_step * viscosity / 12.0
KEEP = 1.0 - 60.0 * A
SLOPE = 1.0 / 12.0

WIDTHS = [16] * PROBES + [16, 14, 12, 10] + [8]
LANES = [sum(WIDTHS[:f]) for f in range(len(WIDTHS))]
PACK_ROWS = [0, 16, 30, 42, 52]
MESH = pl.DeviceIdType.MESH


def left(x, by):
    return pltpu.roll(x, by % 128, 1)


def lanes(rows):
    return lax.broadcasted_iota(jnp.int32, (rows, 128), 1)


def kernel(
    heights, probes, cotangent, q_out, p_out,
    hb, ub, cb, send_rows, rows_u, rows_h, send_cols, cols,
    H, U0, U1, U2, U3, AR, AC, BR, BC, PP, PS, MP, M3, N3, Q3, Q2, QR, Q1, M2, M1, M0, W, WK,
    local_sem, send_sem, recv_sem, answer,
):
    gx, gy = lax.axis_index("gx"), lax.axis_index("gy")
    n_gx, n_gy = lax.axis_size("gx"), lax.axis_size("gy")
    core = lax.rem(gx, 2)
    late = lax.rem(lax.div(gx, 2), 2)
    near_gx = gx + 1 - 2 * core
    far_gx = lax.rem(gx - 1 + 2 * core + n_gx, n_gx)
    west, east = lax.rem(gy + n_gy - 1, n_gy), lax.rem(gy + 1, n_gy)
    y = lax.rem(gy, 4)

    def signal(sem, device):
        pl.semaphore_signal(sem, inc=1, device_id=device, device_id_type=MESH)

    greets_far, greets_near, greets_west, greets_east = late == 0, core == 1, y == 0, y < 3
    barrier = pltpu.get_barrier_semaphore()
    far_corners = [(far_gx, west), (far_gx, east)]

    @pl.when(greets_near)
    def _():
        signal(barrier, (near_gx, gy))

    @pl.when(greets_far)
    def _():
        for d in [(far_gx, gy)] + far_corners:
            signal(barrier, d)

    @pl.when(greets_east)
    def _():
        for d in [(gx, east), (near_gx, east)]:
            signal(barrier, d)

    @pl.when(greets_west)
    def _():
        for d in [(gx, west), (near_gx, west)]:
            signal(barrier, d)

    loads = [
        pltpu.make_async_copy(heights, hb, local_sem.at[0]),
        pltpu.make_async_copy(cotangent, cb, local_sem.at[1]),
        pltpu.make_async_copy(probes, ub, local_sem.at[2]),
    ]
    for c in loads:
        c.start()

    def taps(rows, one, two, sign):
        into = lax.broadcasted_iota(jnp.int32, (rows, 128), 0)
        off = lax.rem(into, 128) - lax.broadcasted_iota(jnp.int32, (rows, 128), 1)
        value = jnp.where(off == 1, one, 0.0) + jnp.where(off == -1, sign * one, 0.0)
        value = value + jnp.where(off == 2, two, 0.0) + jnp.where(off == -2, sign * two, 0.0)
        return value.astype(jnp.bfloat16)

    W[:, 0:128] = taps(256, 8.0, -1.0, -1.0)
    W[:, 128:256] = taps(256, 16.0, -1.0, 1.0)
    WK[0:256] = taps(256, 16.0, -1.0, 1.0)
    WK[256:512] = taps(256, -8.0, 1.0, -1.0)

    near_edge, far_edge = 1 - core, core
    near_halo, far_halo = 1 - core, core

    def copy(src, dst, s, d):
        return pltpu.make_async_remote_copy(
            src_ref=src, dst_ref=dst, send_sem=send_sem.at[s], recv_sem=recv_sem.at[s],
            device_id=d, device_id_type=MESH,
        )

    def row_start(edge):
        return pl.multiple_of(edge * (ROWS - REACH), 16)

    def halo_start(halo):
        return pl.multiple_of(halo * (SPAN - REACH), 16)

    def u_copy(edge, p, s, d):
        return copy(probes.at[p, pl.ds(row_start(edge), REACH)], rows_u.at[1 - edge, p], s, d)

    def h_copy(edge, s, d):
        part = (slice(None), pl.ds(0, 64))
        return copy(send_rows.at[(edge, *part)], rows_h.at[(1 - edge, *part)], s, d)

    def c_copy(side, s, d):
        return copy(send_cols.at[side], cols.at[1 - side, pl.ds(REACH, ROWS)], s, d)

    def k_copy(side, edge, s, d):
        return copy(
            send_cols.at[side, pl.ds(row_start(edge), REACH)],
            cols.at[1 - side, pl.ds(halo_start(1 - edge), REACH)], s, d,
        )

    far_u = [u_copy(far_edge, p, p, (far_gx, gy)) for p in range(PROBES)]
    far_h = h_copy(far_edge, 4, (far_gx, gy))
    far_k = [k_copy(side, far_edge, 5 + side, far_corners[side]) for side in (0, 1)]
    near_u = [u_copy(near_edge, p, 7 + p, (near_gx, gy)) for p in range(PROBES)]
    near_h = h_copy(near_edge, 11, (near_gx, gy))
    near_k = [k_copy(0, near_edge, 12, (near_gx, west)), k_copy(1, near_edge, 13, (near_gx, east))]
    side_c = [c_copy(0, 14, (gx, west)), c_copy(1, 15, (gx, east))]

    greeters = 3 * late + (1 - core) + jnp.where(y > 0, 2, 0) + jnp.where(y == 3, 2, 0)

    @pl.when(greeters > 0)
    def _():
        pl.semaphore_wait(barrier, greeters)


    @pl.when(late == 1)
    def _():
        for c in far_u[:2]:
            c.start()
        signal(answer.at[0], (far_gx, gy))
        for d in far_corners:
            signal(answer.at[1], d)

    @pl.when(core == 0)
    def _():
        signal(answer.at[2], (near_gx, gy))

    @pl.when(y > 0)
    def _():
        for d in [(gx, west), (near_gx, west)]:
            signal(answer.at[4], d)

    @pl.when(y == 3)
    def _():
        for d in [(gx, east), (near_gx, east)]:
            signal(answer.at[3], d)

    def answered(greeted, which, count):
        @pl.when(greeted)
        def _():
            pl.semaphore_wait(answer.at[which], count)

    def early_sends():
        pl.semaphore_wait(answer.at[0], 1)
        for c in far_u[:2] + [far_h] + far_u[2:]:
            c.start()
        pl.semaphore_wait(answer.at[1], 2)
        for c in far_k:
            c.start()

    answered(greets_near, 2, 1)
    for c in near_u:
        c.start()

    loads[0].wait()
    loads[1].wait()
    for n in range(4):
        cut = slice(128 * n, 128 * n + 128)
        for k in range(STEPS):
            send_rows[0, n, PACK_ROWS[k] : PACK_ROWS[k] + 16] = hb[k, 0:16, cut].astype(jnp.float32)
        send_rows[0, n, 52:60] = cb[0:8, cut]
        for k in reversed(range(STEPS)):
            first = PACK_ROWS[k] - 2 * k
            send_rows[1, n, first : first + 16] = hb[k, 48:64, cut].astype(jnp.float32)
        send_rows[1, n, 52:60] = cb[56:64, cut]
    near_h.start()

    loads[2].wait()
    lane = lanes(ROWS)
    for side in (0, 1):
        packed = None
        for f, (w, o) in enumerate(zip(WIDTHS, LANES)):
            cut = slice(0, 128) if side == 0 else slice(COLS - 128, COLS)
            if f < 4:
                x = ub[f, :, cut]
            elif f < 8:
                x = hb[f - 4, :, cut].astype(jnp.float32)
            else:
                x = cb[:, cut]
            x = left(x, o if side == 0 else o + w)
            packed = x if packed is None else jnp.where(lane < o, packed, x)
        send_cols[side] = packed
    for side, greeted in ((0, greets_west), (1, greets_east)):
        answered(greeted, 3 + side, 2)
        for c in (side_c[side], near_k[side]):
            c.start()

    @pl.when(late == 1)
    def _():
        for c in far_k + [far_h] + far_u[2:]:
            c.start()

    def inner_tiles(store, nat, rows):
        lane = lanes(rows)
        for j, shift in ((1, 40), (2, 64), (3, 88)):
            store(j, jnp.where(lane < shift, left(nat[j - 1], shift), left(nat[j], shift)))
        return left(nat[0], 16), left(nat[3], 112)

    def outer_tiles(store, first, last, before, after, f, rows):
        lane = lanes(rows)
        w, o = WIDTHS[f], LANES[f]
        store(0, jnp.where(lane < 16, left(before, 16 - w - o), first))
        store(4, jnp.where(lane < 112, last, left(after, 112 - o)))

    def place(f):
        return (U0, (f,)) if f < 4 else (H, (f - 4,)) if f < 8 else (PP, (4,))

    def put(f, start, rows):
        ref, lead = place(f)

        def store(j, value):
            ref[(*lead, j, pl.ds(start, rows))] = value

        return store

    def load_own():
        for f in range(9):
            cuts = [slice(128 * n, 128 * n + 128) for n in range(4)]
            if f < 4:
                nat = [ub[f, :, cut] for cut in cuts]
            elif f < 8:
                nat = [hb[f - 4, :, cut].astype(jnp.float32) for cut in cuts]
            else:
                nat = [cb[:, cut] for cut in cuts]
            store = put(f, REACH, ROWS)
            first, last = inner_tiles(store, nat, ROWS)
            store(0, first)
            store(4, last)

    def own_sides():
        before, after = cols[0, REACH : REACH + ROWS], cols[1, REACH : REACH + ROWS]
        for f in range(9):
            ref, lead = place(f)
            mine = slice(REACH, REACH + ROWS)
            outer_tiles(put(f, REACH, ROWS), ref[(*lead, 0, mine)], ref[(*lead, 4, mine)], before, after, f, ROWS)

    def load_halo(halo, fields):
        start = halo_start(halo)
        before, after = cols[0, pl.ds(start, REACH)], cols[1, pl.ds(start, REACH)]
        for f in fields:
            if f < 4:
                nat = [rows_u[halo, f, :, 128 * n : 128 * n + 128] for n in range(4)]
            else:
                k = f - 4
                first = PACK_ROWS[k] - (1 - halo) * (2 * k)
                nat = [rows_h[halo, n, pl.ds(first, REACH)] for n in range(4)]
            store = put(f, start, REACH)
            first, last = inner_tiles(store, nat, REACH)
            outer_tiles(store, first, last, before, after, f, REACH)

    def dot(x, w):
        return jnp.dot(x, w, preferred_element_type=jnp.float32)

    def halves(x):
        high = x.astype(jnp.bfloat16)
        return [high, (x - high.astype(jnp.float32)).astype(jnp.bfloat16)]

    def along(columns, w):
        rows = columns[0][0].shape[0]
        stacked = [jnp.concatenate(sum([halves(x) for x in xs], []), axis=1) for xs in columns]
        out = dot(jnp.concatenate(stacked, axis=0), w)
        return [out[i * rows : i * rows + rows] for i in range(len(columns))]

    def slopes(region):
        for k in range(STEPS):
            start, rows = region(2 * k + 2)
            here = pl.ds(start, rows)
            whole = jnp.concatenate([H[k, j, here].astype(jnp.bfloat16) for j in range(TILES)], axis=0)
            cross = dot(whole, W[0:128, 0:128])
            for j in range(TILES):
                at = lambda d: H[k, j, pl.ds(start + d, rows)]
                AR[k, j, here] = SLOPE * (8.0 * (at(1) - at(-1)) - (at(2) - at(-2)))
                AC[k, j, here] = SLOPE * cross[j * rows : j * rows + rows]

    def over(first, last, batch, body):
        pairs = [(p, j) for p in range(first, last) for j in range(TILES)]
        for i in range(0, len(pairs), batch):
            body(pairs[i : i + batch])

    def tangent(k, source, target, region):
        start, rows = region
        here = pl.ds(start, rows)

        def body(pairs):
            cross = along([[source[p, j, here]] for p, j in pairs], W[:, 0:128] if target is None else W[...])
            for (p, j), c in zip(pairs, cross):
                at = lambda d: source[p, j, pl.ds(start + d, rows)]
                n1, s1, n2, s2 = at(-1), at(1), at(-2), at(2)
                br = 8.0 * (s1 - n1) - (s2 - n2)
                bc = c[:, 0:128]
                if target is None:
                    M3[p, j, here] = PS[STEPS, j, here] * br
                    N3[p, j, here] = PS[STEPS, j, here] * bc
                    continue
                BR[k, p, j, here] = br
                BC[k, p, j, here] = bc
                lap = (16.0 * (n1 + s1) - (n2 + s2)) + c[:, 128:256]
                target[p, j, here] = KEEP * at(0) + A * (
                    lap + AR[k, j, here] * br + AC[k, j, here] * bc
                )

        return body

    def spread(q_at, m_at, cross):
        s = q_at(-1) + q_at(1)
        ring = (s + s) + (m_at(-1) - m_at(1))
        outer = (q_at(-2) + q_at(2)) + (m_at(-2) - m_at(2))
        return KEEP * q_at(0) + A * ((8.0 * ring - outer) + cross)

    def p_flux(region):
        start, rows = region
        here = pl.ds(start, rows)
        for j in range(TILES):
            x = PP[STEPS, j, here]
            PS[STEPS, j, here] = SLOPE * x
            MP[STEPS, j, here] = x * AR[STEPS - 1, j, here]

    def p_step(k, region):
        start, rows = region
        here = pl.ds(start, rows)
        now = [PP[k + 1, j, here] for j in range(TILES)]
        cross = along([[x, x * AC[k, j, here]] for j, x in enumerate(now)], WK[...])
        results = []
        for j in range(TILES):
            q_at = lambda d: PP[k + 1, j, pl.ds(start + d, rows)]
            m_at = lambda d: MP[k + 1, j, pl.ds(start + d, rows)]
            out = spread(q_at, m_at, cross[j])
            if k > 0:
                PP[k, j, here] = out
                PS[k, j, here] = SLOPE * out
                MP[k, j, here] = out * AR[k - 1, j, here]
            results.append(out)
        if k == 0:
            to_natural(p_out, (), results, start, rows)

    def to_natural(ref, lead, tiles, start, rows):
        lane = lanes(rows)
        moved = [left(t, s) for t, s in zip(tiles, (112, 88, 64, 40, 16))]
        first = pl.multiple_of(start - REACH, 16)
        for n, edge in enumerate((100, 76, 52, 28)):
            ref[(*lead, pl.ds(first, rows), slice(128 * n, 128 * n + 128))] = jnp.where(
                lane < edge, moved[n], moved[n + 1]
            )

    def q_first(region):
        start, rows = region
        here = pl.ds(start, rows)

        def body(pairs):
            cross = along([[N3[p, j, here]] for p, j in pairs], WK[256:512])
            for (p, j), c in zip(pairs, cross):
                m_at = lambda d: M3[p, j, pl.ds(start + d, rows)]
                out = A * ((8.0 * (m_at(-1) - m_at(1)) - (m_at(-2) - m_at(2))) + c)
                Q3[p, j, here] = out
                M2[p, j, here] = out * AR[2, j, here] + PS[3, j, here] * BR[2, p, j, here]

        return body

    def q_step(k, source, flux, target, next_flux, region):
        start, rows = region
        here = pl.ds(start, rows)

        def body(pairs):
            def operands(p, j):
                x = source[p, j, here]
                return [x, x * AC[k, j, here] + PS[k + 1, j, here] * BC[k, p, j, here]]

            cross = along([operands(p, j) for p, j in pairs], WK[...])
            results = []
            for (p, j), c in zip(pairs, cross):
                q_at = lambda d: source[p, j, pl.ds(start + d, rows)]
                m_at = lambda d: flux[p, j, pl.ds(start + d, rows)]
                out = spread(q_at, m_at, c)
                if target is not None:
                    target[p, j, here] = out
                if next_flux is not None:
                    next_flux[p, j, here] = out * AR[k - 1, j, here] + PS[k, j, here] * BR[k - 1, p, j, here]
                results.append(out)
            if target is None:
                for i in range(0, len(pairs), TILES):
                    to_natural(q_out, (pairs[i][0],), results[i : i + TILES], start, rows)

        return body

    def refresh(region):
        start, rows = region

        def body(pairs):
            here = pl.ds(start, rows)
            lane = lanes(rows)
            for p, j in pairs:
                x = Q2[p, j, here]
                if j > 0:
                    x = jnp.where(lane < 12, left(Q2[p, j - 1, here], -104), x)
                if j < TILES - 1:
                    x = jnp.where(lane >= 116, left(Q2[p, j + 1, here], 104), x)
                QR[p, j, here] = x
                M1[p, j, here] = x * AR[1, j, here] + PS[2, j, here] * BR[1, p, j, here]

        return body

    def shared(region):
        slopes(region)
        p_flux(region(8))
        for k in reversed(range(STEPS)):
            p_step(k, region(16 - 2 * k))

    def sweep(region, first, last, batch):
        run = functools.partial(over, first, last, batch)
        run(tangent(0, U0, U1, region(2)))
        run(tangent(1, U1, U2, region(4)))
        run(tangent(2, U2, U3, region(6)))
        run(tangent(3, U3, None, region(8)))
        run(q_first(region(10)))
        run(q_step(2, Q3, M2, Q2, None, region(12)))
        run(refresh(region(12)))
        run(q_step(1, QR, M1, Q1, M0, region(14)))
        run(q_step(0, Q1, M0, None, None, region(16)))

    def main_region(margin):
        rows = (80 - 2 * margin + 15) // 16 * 16
        if margin == 16:
            return pl.multiple_of(32 - 16 * core, 16), rows
        return (1 - core) * (SPAN - margin - rows) + core * margin, rows

    load_own()

    @pl.when((late == 0) & (gx > 0))
    def _():
        early_sends()

    for c in near_u + [near_h] + near_k + side_c:
        c.wait_recv()
    own_sides()
    load_halo(near_halo, range(9))
    shared(main_region)

    @pl.when(gx == 0)
    def _():
        early_sends()

    sweep(main_region, 0, PROBES, 5)

    def wedge_region(margin):
        if margin == 16:
            return pl.multiple_of(16 + 48 * core, 16), REACH
        return (1 - core) * margin + core * (80 - margin), REACH

    far_h.wait_recv()
    for c in far_k:
        c.wait_recv()
    load_halo(far_halo, range(4, 9))
    shared(wedge_region)
    for c in far_u:
        c.wait_recv()
    load_halo(far_halo, range(4))
    sweep(wedge_region, 0, PROBES, 10)

    for c in far_u + [far_h] + far_k + near_u + [near_h] + near_k + side_c:
        c.wait_send()


def store_all(q, p, q_out, p_out, sem):
    copies = [
        pltpu.make_async_copy(q, q_out, sem.at[0]),
        pltpu.make_async_copy(p, p_out, sem.at[1]),
    ]
    for c in copies:
        c.start()
    for c in copies:
        c.wait()


def on_device(heights, probes, cotangent):
    f32 = jnp.float32
    probe = pltpu.VMEM((PROBES, TILES, SPAN, 128), f32)
    steps = pltpu.VMEM((STEPS + 1, TILES, SPAN, 128), f32)
    slope = pltpu.VMEM((3, PROBES, TILES, SPAN, 128), f32)
    q, p = pl.pallas_call(
        kernel,
        out_shape=[pltpu.VMEM((PROBES, ROWS, COLS), f32), pltpu.VMEM((ROWS, COLS), f32)],
        in_specs=[pl.BlockSpec(memory_space=pl.ANY)] * 3,
        out_specs=[pl.BlockSpec(memory_space=pltpu.VMEM)] * 2,
        scratch_shapes=[
            pltpu.VMEM((STEPS, ROWS, COLS), jnp.bfloat16),
            pltpu.VMEM((PROBES, ROWS, COLS), f32),
            pltpu.VMEM((ROWS, COLS), f32),
            pltpu.VMEM((2, 4, 72, 128), f32),
            pltpu.VMEM((2, PROBES, REACH, COLS), f32),
            pltpu.VMEM((2, 4, 72, 128), f32),
            pltpu.VMEM((2, ROWS, 128), f32),
            pltpu.VMEM((2, SPAN, 128), f32),
            probe,
            probe, probe, probe, probe,
            probe, probe,
            slope, slope,
            steps, steps, steps,
            probe, probe, probe, probe, probe, probe, probe, probe, probe,
            pltpu.VMEM((256, 256), jnp.bfloat16),
            pltpu.VMEM((512, 128), jnp.bfloat16),
            pltpu.SemaphoreType.DMA((3,)),
            pltpu.SemaphoreType.DMA((16,)),
            pltpu.SemaphoreType.DMA((16,)),
            pltpu.SemaphoreType.REGULAR((5,)),
        ],
        compiler_params=pltpu.CompilerParams(
            collective_id=0, has_side_effects=True, vmem_limit_bytes=56 * 2**20
        ),
    )(heights, probes, cotangent)
    return pl.pallas_call(
        store_all,
        out_shape=[jax.ShapeDtypeStruct(q.shape, f32), jax.ShapeDtypeStruct(p.shape, f32)],
        in_specs=[pl.BlockSpec(memory_space=pltpu.VMEM)] * 2,
        out_specs=[pl.BlockSpec(memory_space=pl.ANY)] * 2,
        scratch_shapes=[pltpu.SemaphoreType.DMA((2,))],
    )(
        pltpu.with_memory_space_constraint(q, pltpu.VMEM),
        pltpu.with_memory_space_constraint(p, pltpu.VMEM),
    )


def solution(mesh):
    in_specs = (P(None, "gx", "gy"), P(None, "gx", "gy"), P("gx", "gy"))
    out_specs = (P(None, "gx", "gy"), P("gx", "gy"))
    return jax.shard_map(
        on_device, mesh=mesh, in_specs=in_specs, out_specs=out_specs, check_vma=False
    )
```

```python
import functools

import jax
import jax.numpy as jnp
from jax import lax
from jax.experimental import pallas as pl
from jax.experimental.pallas import tpu as pltpu
from jax.sharding import PartitionSpec as P

STEPS = 4
PROBES = 4
TILES = 5
REACH = 16
ROWS, COLS = 64, 512
SPAN = ROWS + 2 * REACH

time_step = 0.05
viscosity = 3.0
coupling = 3.0
A = time_step * viscosity / 12.0
KEEP = 1.0 - 60.0 * A
SLOPE = 1.0 / 12.0

WIDTHS = [16] * PROBES + [16, 14, 12, 10] + [8]
LANES = [sum(WIDTHS[:f]) for f in range(len(WIDTHS))]
PACK_ROWS = [0, 16, 30, 42, 52]
MESH = pl.DeviceIdType.MESH


def left(x, by):
    return pltpu.roll(x, by % 128, 1)


def lanes(rows):
    return lax.broadcasted_iota(jnp.int32, (rows, 128), 1)


def kernel(
    heights, probes, cotangent, q_out, p_out,
    hb, ub, cb, send_rows, rows_u, rows_h, send_cols, cols,
    H, U0, U1, U2, U3, AR, AC, BR, BC, PP, PS, MP, M3, N3, Q3, Q2, QR, Q1, M2, M1, M0, W, WK,
    local_sem, send_sem, recv_sem, answer,
):
    gx, gy = lax.axis_index("gx"), lax.axis_index("gy")
    n_gx, n_gy = lax.axis_size("gx"), lax.axis_size("gy")
    core = lax.rem(gx, 2)
    near_gx = gx + 1 - 2 * core
    far_gx = lax.rem(gx - 1 + 2 * core + n_gx, n_gx)
    west, east = lax.rem(gy + n_gy - 1, n_gy), lax.rem(gy + 1, n_gy)

    def signal(sem, device):
        pl.semaphore_signal(sem, inc=1, device_id=device, device_id_type=MESH)

    first_row, last_row = gx == 0, gx == n_gx - 1
    y = lax.rem(gy, 4)
    asks_west = last_row & (y == 0)
    answers = [last_row & (y == 3), (gx == n_gx - 2) & (y == 3)]
    barrier = pltpu.get_barrier_semaphore()
    far, western, eastern = (far_gx, gy), [(gx, west), (near_gx, west)], [(gx, east), (near_gx, east)]
    corners = [(far_gx, west), (far_gx, east)]

    @pl.when(jnp.logical_not(last_row))
    def _():
        signal(barrier, far)

    @pl.when(first_row)
    def _():
        for d in corners:
            signal(barrier, d)

    for d in [(near_gx, gy)] + western:
        signal(barrier, d)
    for d, special in zip(eastern, answers):

        @pl.when(jnp.logical_not(special))
        def _():
            signal(barrier, d)

    loads = [
        pltpu.make_async_copy(heights, hb, local_sem.at[0]),
        pltpu.make_async_copy(cotangent, cb, local_sem.at[1]),
        pltpu.make_async_copy(probes, ub, local_sem.at[2]),
    ]
    for c in loads:
        c.start()

    def taps(rows, one, two, sign):
        into = lax.broadcasted_iota(jnp.int32, (rows, 128), 0)
        off = lax.rem(into, 128) - lax.broadcasted_iota(jnp.int32, (rows, 128), 1)
        value = jnp.where(off == 1, one, 0.0) + jnp.where(off == -1, sign * one, 0.0)
        value = value + jnp.where(off == 2, two, 0.0) + jnp.where(off == -2, sign * two, 0.0)
        return value.astype(jnp.bfloat16)

    W[:, 0:128] = taps(256, 8.0, -1.0, -1.0)
    W[:, 128:256] = taps(256, 16.0, -1.0, 1.0)
    WK[0:256] = taps(256, 16.0, -1.0, 1.0)
    WK[256:512] = taps(256, -8.0, 1.0, -1.0)

    near_edge, far_edge = 1 - core, core
    near_halo, far_halo = 1 - core, core

    def copy(src, dst, s, d):
        return pltpu.make_async_remote_copy(
            src_ref=src, dst_ref=dst, send_sem=send_sem.at[s], recv_sem=recv_sem.at[s],
            device_id=d, device_id_type=MESH,
        )

    def row_start(edge):
        return pl.multiple_of(edge * (ROWS - REACH), 16)

    def halo_start(halo):
        return pl.multiple_of(halo * (SPAN - REACH), 16)

    def u_copy(edge, p, s, d):
        return copy(probes.at[p, pl.ds(row_start(edge), REACH)], rows_u.at[1 - edge, p], s, d)

    def h_copy(edge, s, d):
        part = (slice(None), pl.ds(0, 64))
        return copy(send_rows.at[(edge, *part)], rows_h.at[(1 - edge, *part)], s, d)

    def c_copy(side, s, d):
        return copy(send_cols.at[side], cols.at[1 - side, pl.ds(REACH, ROWS)], s, d)

    def k_copy(side, s, d):
        return copy(
            send_cols.at[side, pl.ds(row_start(near_edge), REACH)],
            cols.at[1 - side, pl.ds(halo_start(1 - near_edge), REACH)], s, d,
        )

    def direct(side, s):
        return copy(
            send_cols.at[side, pl.ds(row_start(far_edge), REACH)],
            cols.at[1 - side, pl.ds(halo_start(1 - far_edge), REACH)], s, corners[side],
        )

    def pass_on(side, s):
        return copy(
            cols.at[side, pl.ds(pl.multiple_of(REACH + row_start(far_edge), 16), REACH)],
            cols.at[side, pl.ds(halo_start(1 - far_edge), REACH)], s, far,
        )

    far_u = [u_copy(far_edge, p, p, far) for p in range(PROBES)]
    far_h = h_copy(far_edge, 4, far)
    far_k = [pass_on(side, 5 + side) for side in (0, 1)]
    direct_k = [direct(side, 5 + side) for side in (0, 1)]
    near_u = [u_copy(near_edge, p, 7 + p, (near_gx, gy)) for p in range(PROBES)]
    near_h = h_copy(near_edge, 11, (near_gx, gy))
    near_k = [k_copy(0, 12, western[1]), k_copy(1, 13, eastern[1])]
    side_c = [c_copy(0, 14, western[0]), c_copy(1, 15, eastern[0])]
    bulk = far_u[:2] + [far_h] + far_u[2:]

    loads[0].wait()
    loads[1].wait()
    for n in range(4):
        cut = slice(128 * n, 128 * n + 128)
        for k in range(STEPS):
            send_rows[0, n, PACK_ROWS[k] : PACK_ROWS[k] + 16] = hb[k, 0:16, cut].astype(jnp.float32)
        send_rows[0, n, 52:60] = cb[0:8, cut]
        for k in reversed(range(STEPS)):
            first = PACK_ROWS[k] - 2 * k
            send_rows[1, n, first : first + 16] = hb[k, 48:64, cut].astype(jnp.float32)
        send_rows[1, n, 52:60] = cb[56:64, cut]

    loads[2].wait()
    lane = lanes(ROWS)
    for side in (0, 1):
        packed = None
        for f, (w, o) in enumerate(zip(WIDTHS, LANES)):
            cut = slice(0, 128) if side == 0 else slice(COLS - 128, COLS)
            if f < 4:
                x = ub[f, :, cut]
            elif f < 8:
                x = hb[f - 4, :, cut].astype(jnp.float32)
            else:
                x = cb[:, cut]
            x = left(x, o if side == 0 else o + w)
            packed = x if packed is None else jnp.where(lane < o, packed, x)
        send_cols[side] = packed

    pl.semaphore_wait(barrier, 5 + jnp.where(first_row, 0, jnp.where(last_row, 3, 1)) - jnp.where(asks_west, 2, 0))

    @pl.when(last_row)
    def _():
        for d in [far] + corners:
            signal(answer.at[0], d)
        for c in direct_k:
            c.start()

    for d, special in zip(eastern, answers):

        @pl.when(special)
        def _():
            signal(answer.at[1], d)

    for c in near_u + [near_h, side_c[1], near_k[1]]:
        c.start()

    @pl.when(jnp.logical_not(asks_west))
    def _():
        for c in [side_c[0], near_k[0]]:
            c.start()

    @pl.when(jnp.logical_not(first_row))
    def _():
        for c in bulk:
            c.start()

    def inner_tiles(store, nat, rows):
        lane = lanes(rows)
        for j, shift in ((1, 40), (2, 64), (3, 88)):
            store(j, jnp.where(lane < shift, left(nat[j - 1], shift), left(nat[j], shift)))

    def outer_tiles(store, first, last, before, after, f, rows):
        lane = lanes(rows)
        w, o = WIDTHS[f], LANES[f]
        store(0, jnp.where(lane < 16, left(before, 16 - w - o), left(first, 16)))
        store(4, jnp.where(lane < 112, left(last, 112), left(after, 112 - o)))

    def put(f, start, rows):
        ref, lead = (U0, (f,)) if f < 4 else (H, (f - 4,)) if f < 8 else (PP, (4,))

        def store(j, value):
            ref[(*lead, j, pl.ds(start, rows))] = value

        return store

    def own(f, n):
        cut = slice(128 * n, 128 * n + 128)
        return ub[f, :, cut] if f < 4 else hb[f - 4, :, cut].astype(jnp.float32) if f < 8 else cb[:, cut]

    def lay_own(inner):
        for f in range(9):
            store = put(f, REACH, ROWS)
            if inner:
                inner_tiles(store, [own(f, n) for n in range(4)], ROWS)
            else:
                mine = slice(REACH, REACH + ROWS)
                outer_tiles(store, own(f, 0), own(f, 3), cols[0, mine], cols[1, mine], f, ROWS)

    def lay_halo(halo, fields, inner, outer):
        start = halo_start(halo)
        for f in fields:

            def part(n):
                if f < 4:
                    return rows_u[halo, f, :, 128 * n : 128 * n + 128]
                k = f - 4
                return rows_h[halo, n, pl.ds(PACK_ROWS[k] - (1 - halo) * (2 * k), REACH)]

            store = put(f, start, REACH)
            if inner:
                inner_tiles(store, [part(n) for n in range(4)], REACH)
            if outer:
                sides = [cols[side, pl.ds(start, REACH)] for side in (0, 1)]
                outer_tiles(store, part(0), part(3), *sides, f, REACH)

    def dot(x, w):
        return jnp.dot(x, w, preferred_element_type=jnp.float32)

    def halves(x):
        high = x.astype(jnp.bfloat16)
        return [high, (x - high.astype(jnp.float32)).astype(jnp.bfloat16)]

    def along(columns, w):
        rows = columns[0][0].shape[0]
        stacked = [jnp.concatenate(sum([halves(x) for x in xs], []), axis=1) for xs in columns]
        out = dot(jnp.concatenate(stacked, axis=0), w)
        return [out[i * rows : i * rows + rows] for i in range(len(columns))]

    def slopes(region, tiles):
        for k in range(STEPS):
            start, rows = region(2 * k + 2)
            here = pl.ds(start, rows)
            whole = jnp.concatenate([H[k, j, here].astype(jnp.bfloat16) for j in tiles], axis=0)
            cross = dot(whole, W[0:128, 0:128])
            for i, j in enumerate(tiles):
                at = lambda d: H[k, j, pl.ds(start + d, rows)]
                AR[k, j, here] = SLOPE * (8.0 * (at(1) - at(-1)) - (at(2) - at(-2)))
                AC[k, j, here] = SLOPE * cross[i * rows : i * rows + rows]

    def over(probes_of, tiles, batch, body):
        pairs = [(p, j) for p in probes_of for j in tiles]
        for i in range(0, len(pairs), batch):
            body(pairs[i : i + batch])

    def tangent(k, source, target, region):
        start, rows = region
        here = pl.ds(start, rows)

        def body(pairs):
            cross = along([[source[p, j, here]] for p, j in pairs], W[:, 0:128] if target is None else W[...])
            for (p, j), c in zip(pairs, cross):
                at = lambda d: source[p, j, pl.ds(start + d, rows)]
                n1, s1, n2, s2 = at(-1), at(1), at(-2), at(2)
                br = 8.0 * (s1 - n1) - (s2 - n2)
                bc = c[:, 0:128]
                if target is None:
                    M3[p, j, here] = PS[STEPS, j, here] * br
                    N3[p, j, here] = PS[STEPS, j, here] * bc
                    continue
                BR[k, p, j, here] = br
                BC[k, p, j, here] = bc
                lap = (16.0 * (n1 + s1) - (n2 + s2)) + c[:, 128:256]
                target[p, j, here] = KEEP * at(0) + A * (
                    lap + AR[k, j, here] * br + AC[k, j, here] * bc
                )

        return body

    def spread(q_at, m_at, cross):
        s = q_at(-1) + q_at(1)
        ring = (s + s) + (m_at(-1) - m_at(1))
        outer = (q_at(-2) + q_at(2)) + (m_at(-2) - m_at(2))
        return KEEP * q_at(0) + A * ((8.0 * ring - outer) + cross)

    def p_flux(region, tiles):
        start, rows = region
        here = pl.ds(start, rows)
        for j in tiles:
            x = PP[STEPS, j, here]
            PS[STEPS, j, here] = SLOPE * x
            MP[STEPS, j, here] = x * AR[STEPS - 1, j, here]

    def p_step(k, region, tiles):
        start, rows = region
        here = pl.ds(start, rows)
        cross = along([[PP[k + 1, j, here], PP[k + 1, j, here] * AC[k, j, here]] for j in tiles], WK[...])
        results = []
        for j, c in zip(tiles, cross):
            q_at = lambda d: PP[k + 1, j, pl.ds(start + d, rows)]
            m_at = lambda d: MP[k + 1, j, pl.ds(start + d, rows)]
            out = spread(q_at, m_at, c)
            if k > 0:
                PP[k, j, here] = out
                PS[k, j, here] = SLOPE * out
                MP[k, j, here] = out * AR[k - 1, j, here]
            results.append(out)
        if k == 0:
            to_natural(p_out, (), results, start, rows)

    def to_natural(ref, lead, tiles, start, rows):
        lane = lanes(rows)
        moved = [left(t, s) for t, s in zip(tiles, (112, 88, 64, 40, 16))]
        first = pl.multiple_of(start - REACH, 16)
        for n, edge in enumerate((100, 76, 52, 28)):
            ref[(*lead, pl.ds(first, rows), slice(128 * n, 128 * n + 128))] = jnp.where(
                lane < edge, moved[n], moved[n + 1]
            )

    def q_first(region):
        start, rows = region
        here = pl.ds(start, rows)

        def body(pairs):
            cross = along([[N3[p, j, here]] for p, j in pairs], WK[256:512])
            for (p, j), c in zip(pairs, cross):
                m_at = lambda d: M3[p, j, pl.ds(start + d, rows)]
                out = A * ((8.0 * (m_at(-1) - m_at(1)) - (m_at(-2) - m_at(2))) + c)
                Q3[p, j, here] = out
                M2[p, j, here] = out * AR[2, j, here] + PS[3, j, here] * BR[2, p, j, here]

        return body

    def q_step(k, source, flux, target, next_flux, region):
        start, rows = region
        here = pl.ds(start, rows)

        def body(pairs):
            def operands(p, j):
                x = source[p, j, here]
                return [x, x * AC[k, j, here] + PS[k + 1, j, here] * BC[k, p, j, here]]

            cross = along([operands(p, j) for p, j in pairs], WK[...])
            results = []
            for (p, j), c in zip(pairs, cross):
                q_at = lambda d: source[p, j, pl.ds(start + d, rows)]
                m_at = lambda d: flux[p, j, pl.ds(start + d, rows)]
                out = spread(q_at, m_at, c)
                if target is not None:
                    target[p, j, here] = out
                if next_flux is not None:
                    next_flux[p, j, here] = out * AR[k - 1, j, here] + PS[k, j, here] * BR[k - 1, p, j, here]
                results.append(out)
            if target is None:
                for i in range(0, len(pairs), TILES):
                    to_natural(q_out, (pairs[i][0],), results[i : i + TILES], start, rows)

        return body

    def refresh(region):
        start, rows = region

        def body(pairs):
            here = pl.ds(start, rows)
            lane = lanes(rows)
            for p, j in pairs:
                x = Q2[p, j, here]
                if j > 0:
                    x = jnp.where(lane < 12, left(Q2[p, j - 1, here], -104), x)
                if j < TILES - 1:
                    x = jnp.where(lane >= 116, left(Q2[p, j + 1, here], 104), x)
                QR[p, j, here] = x
                M1[p, j, here] = x * AR[1, j, here] + PS[2, j, here] * BR[1, p, j, here]

        return body

    everyone, all_tiles = tuple(range(PROBES)), range(TILES)

    def shared(region, tiles):
        slopes(region, tiles)
        p_flux(region(8), tiles)
        for k in (3, 2, 1):
            p_step(k, region(16 - 2 * k), tiles)

    def sweep(region, tiles, batch, which=everyone):
        run = functools.partial(over, which, tiles, batch)
        run(tangent(0, U0, U1, region(2)))
        run(tangent(1, U1, U2, region(4)))
        run(tangent(2, U2, U3, region(6)))
        run(tangent(3, U3, None, region(8)))
        run(q_first(region(10)))
        run(q_step(2, Q3, M2, Q2, None, region(12)))

    def finish(region, batch, which=everyone):
        run = functools.partial(over, which, all_tiles, batch)
        run(refresh(region(12)))
        run(q_step(1, QR, M1, Q1, M0, region(14)))
        run(q_step(0, Q1, M0, None, None, region(16)))

    def main_region(margin):
        rows = (80 - 2 * margin + 15) // 16 * 16
        if margin == 16:
            return pl.multiple_of(32 - 16 * core, 16), rows
        return (1 - core) * (SPAN - margin - rows) + core * margin, rows

    lay_own(True)

    @pl.when(asks_west)
    def _():
        pl.semaphore_wait(answer.at[1], 2)
        for c in [side_c[0], near_k[0]]:
            c.start()

    for c in near_u + [near_h]:
        c.wait_recv()
    lay_halo(near_halo, range(9), True, False)
    shared(main_region, (1, 2, 3))
    sweep(main_region, (1, 2, 3), 6)

    @pl.when(first_row)
    def _():
        pl.semaphore_wait(answer.at[0], 3)
        for c in direct_k + bulk:
            c.start()

    for c in side_c:
        c.wait_recv()

    @pl.when(jnp.logical_not(first_row | last_row))
    def _():
        for c in far_k:
            c.start()

    lay_own(False)
    for c in near_k:
        c.wait_recv()
    lay_halo(near_halo, range(9), False, True)
    shared(main_region, (0, 4))
    sweep(main_region, (0, 4), 4)
    p_step(0, main_region(16), all_tiles)
    finish(main_region, 5)

    def wedge_region(margin):
        if margin == 16:
            return pl.multiple_of(16 + 48 * core, 16), REACH
        return (1 - core) * margin + core * (80 - margin), REACH

    far_h.wait_recv()
    for c in far_k:
        c.wait_recv()
    lay_halo(far_halo, range(4, 9), True, True)
    shared(wedge_region, all_tiles)
    p_step(0, wedge_region(16), all_tiles)
    for c in far_u:
        c.wait_recv()
    lay_halo(far_halo, everyone, True, True)
    sweep(wedge_region, all_tiles, 10)
    finish(wedge_region, 10)

    for c in far_u + [far_h] + far_k + near_u + [near_h] + near_k + side_c:
        c.wait_send()


def store_all(q, p, q_out, p_out, sem):
    copies = [
        pltpu.make_async_copy(q, q_out, sem.at[0]),
        pltpu.make_async_copy(p, p_out, sem.at[1]),
    ]
    for c in copies:
        c.start()
    for c in copies:
        c.wait()


def on_device(heights, probes, cotangent):
    f32 = jnp.float32
    probe = pltpu.VMEM((PROBES, TILES, SPAN, 128), f32)
    steps = pltpu.VMEM((STEPS + 1, TILES, SPAN, 128), f32)
    slope = pltpu.VMEM((3, PROBES, TILES, SPAN, 128), f32)
    q, p = pl.pallas_call(
        kernel,
        out_shape=[pltpu.VMEM((PROBES, ROWS, COLS), f32), pltpu.VMEM((ROWS, COLS), f32)],
        in_specs=[pl.BlockSpec(memory_space=pl.ANY)] * 3,
        out_specs=[pl.BlockSpec(memory_space=pltpu.VMEM)] * 2,
        scratch_shapes=[
            pltpu.VMEM((STEPS, ROWS, COLS), jnp.bfloat16),
            pltpu.VMEM((PROBES, ROWS, COLS), f32),
            pltpu.VMEM((ROWS, COLS), f32),
            pltpu.VMEM((2, 4, 72, 128), f32),
            pltpu.VMEM((2, PROBES, REACH, COLS), f32),
            pltpu.VMEM((2, 4, 72, 128), f32),
            pltpu.VMEM((2, ROWS, 128), f32),
            pltpu.VMEM((2, SPAN, 128), f32),
            probe,
            probe, probe, probe, probe,
            probe, probe,
            slope, slope,
            steps, steps, steps,
            probe, probe, probe, probe, probe, probe, probe, probe, probe,
            pltpu.VMEM((256, 256), jnp.bfloat16),
            pltpu.VMEM((512, 128), jnp.bfloat16),
            pltpu.SemaphoreType.DMA((3,)),
            pltpu.SemaphoreType.DMA((16,)),
            pltpu.SemaphoreType.DMA((16,)),
            pltpu.SemaphoreType.REGULAR((2,)),
        ],
        compiler_params=pltpu.CompilerParams(
            collective_id=0, has_side_effects=True, vmem_limit_bytes=56 * 2**20
        ),
    )(heights, probes, cotangent)
    return pl.pallas_call(
        store_all,
        out_shape=[jax.ShapeDtypeStruct(q.shape, f32), jax.ShapeDtypeStruct(p.shape, f32)],
        in_specs=[pl.BlockSpec(memory_space=pltpu.VMEM)] * 2,
        out_specs=[pl.BlockSpec(memory_space=pl.ANY)] * 2,
        scratch_shapes=[pltpu.SemaphoreType.DMA((2,))],
    )(
        pltpu.with_memory_space_constraint(q, pltpu.VMEM),
        pltpu.with_memory_space_constraint(p, pltpu.VMEM),
    )


def solution(mesh):
    in_specs = (P(None, "gx", "gy"), P(None, "gx", "gy"), P("gx", "gy"))
    out_specs = (P(None, "gx", "gy"), P("gx", "gy"))
    return jax.shard_map(
        on_device, mesh=mesh, in_specs=in_specs, out_specs=out_specs, check_vma=False
    )
```

```python
import functools

import jax
import jax.numpy as jnp
from jax import lax
from jax.experimental import pallas as pl
from jax.experimental.pallas import tpu as pltpu
from jax.sharding import PartitionSpec as P

STEPS = 4
PROBES = 4
TILES = 5
REACH = 16
ROWS, COLS = 64, 512
SPAN = ROWS + 2 * REACH

time_step = 0.05
viscosity = 3.0
coupling = 3.0
A = time_step * viscosity / 12.0
KEEP = 1.0 - 60.0 * A
SLOPE = 1.0 / 12.0

WIDTHS = [16] * PROBES + [16, 14, 12, 10] + [8]
LANES = [sum(WIDTHS[:f]) for f in range(len(WIDTHS))]
PACK_ROWS = [0, 16, 30, 42, 52]
MESH = pl.DeviceIdType.MESH


def left(x, by):
    return pltpu.roll(x, by % 128, 1)


def aligned(x):
    return x if isinstance(x, int) else pl.multiple_of(x, 16)


def lanes(rows):
    return lax.broadcasted_iota(jnp.int32, (rows, 128), 1)


def kernel(
    heights, probes, cotangent, q_out, p_out,
    hb, ub, cb, send_rows, rows_u, rows_h, send_cols, cols,
    H, U0, U1, U2, U3, AR, AC, BR, BC, PP, PS, MP, M3, N3, Q3, Q2, QR, Q1, M2, M1, M0, W, WK,
    local_sem, send_sem, recv_sem, answer,
):
    gx, gy = lax.axis_index("gx"), lax.axis_index("gy")
    n_gx, n_gy = lax.axis_size("gx"), lax.axis_size("gy")
    core = lax.rem(gx, 2)
    near_gx = gx + 1 - 2 * core
    far_gx = lax.rem(gx - 1 + 2 * core + n_gx, n_gx)
    west, east = lax.rem(gy + n_gy - 1, n_gy), lax.rem(gy + 1, n_gy)

    def signal(sem, device):
        pl.semaphore_signal(sem, inc=1, device_id=device, device_id_type=MESH)

    first_row, last_row = gx == 0, gx == n_gx - 1
    y = lax.rem(gy, 4)
    place_of_four = jnp.where(gx < n_gx - 2, lax.rem(gx, 4), -1)
    asks_west = (last_row | (place_of_four == 2)) & (y == 0)
    answers = [
        (last_row | (place_of_four == 2)) & (y == 3),
        ((gx == n_gx - 2) | (place_of_four == 3)) & (y == 3),
    ]
    barrier = pltpu.get_barrier_semaphore()
    far, western, eastern = (far_gx, gy), [(gx, west), (near_gx, west)], [(gx, east), (near_gx, east)]
    corners = [(far_gx, west), (far_gx, east)]

    @pl.when(jnp.logical_not(last_row))
    def _():
        signal(barrier, far)

    @pl.when(first_row)
    def _():
        for d in corners:
            signal(barrier, d)

    for d in [(near_gx, gy)] + western:
        signal(barrier, d)
    for d, special in zip(eastern, answers):

        @pl.when(jnp.logical_not(special))
        def _():
            signal(barrier, d)

    loads = [
        pltpu.make_async_copy(heights, hb, local_sem.at[0]),
        pltpu.make_async_copy(cotangent, cb, local_sem.at[1]),
        pltpu.make_async_copy(probes, ub, local_sem.at[2]),
    ]
    for c in loads:
        c.start()

    def taps(rows, one, two, sign):
        into = lax.broadcasted_iota(jnp.int32, (rows, 128), 0)
        off = lax.rem(into, 128) - lax.broadcasted_iota(jnp.int32, (rows, 128), 1)
        value = jnp.where(off == 1, one, 0.0) + jnp.where(off == -1, sign * one, 0.0)
        value = value + jnp.where(off == 2, two, 0.0) + jnp.where(off == -2, sign * two, 0.0)
        return value.astype(jnp.bfloat16)

    W[:, 0:128] = taps(256, 8.0, -1.0, -1.0)
    W[:, 128:256] = taps(256, 16.0, -1.0, 1.0)
    WK[0:256] = taps(256, 16.0, -1.0, 1.0)
    WK[256:512] = taps(256, -8.0, 1.0, -1.0)

    near_edge, far_edge = 1 - core, core
    def copy(src, dst, s, d):
        return pltpu.make_async_remote_copy(
            src_ref=src, dst_ref=dst, send_sem=send_sem.at[s], recv_sem=recv_sem.at[s],
            device_id=d, device_id_type=MESH,
        )

    def row_start(edge):
        return pl.multiple_of(edge * (ROWS - REACH), 16)

    def halo_start(halo):
        return aligned(halo * (SPAN - REACH))

    def u_copy(edge, p, s, d):
        return copy(ub.at[p, pl.ds(row_start(edge), REACH)], rows_u.at[1 - edge, p], s, d)

    def h_copy(edge, s, d):
        part = (slice(None), pl.ds(0, 64))
        return copy(send_rows.at[(edge, *part)], rows_h.at[(1 - edge, *part)], s, d)

    def c_copy(side, s, d):
        return copy(send_cols.at[side], cols.at[1 - side, pl.ds(REACH, ROWS)], s, d)

    def k_copy(side, s, d):
        return copy(
            send_cols.at[side, pl.ds(row_start(near_edge), REACH)],
            cols.at[1 - side, pl.ds(halo_start(1 - near_edge), REACH)], s, d,
        )

    def direct(side, s):
        return copy(
            send_cols.at[side, pl.ds(row_start(far_edge), REACH)],
            cols.at[1 - side, pl.ds(halo_start(1 - far_edge), REACH)], s, corners[side],
        )

    def pass_on(side, s):
        return copy(
            cols.at[side, pl.ds(pl.multiple_of(REACH + row_start(far_edge), 16), REACH)],
            cols.at[side, pl.ds(halo_start(1 - far_edge), REACH)], s, far,
        )

    far_u = [u_copy(far_edge, p, p, far) for p in range(PROBES)]
    far_h = h_copy(far_edge, 4, far)
    far_k = [pass_on(side, 5 + side) for side in (0, 1)]
    direct_k = [direct(side, 5 + side) for side in (0, 1)]
    near_u = [u_copy(near_edge, p, 7 + p, (near_gx, gy)) for p in range(PROBES)]
    near_h = h_copy(near_edge, 11, (near_gx, gy))
    near_k = [k_copy(0, 12, western[1]), k_copy(1, 13, eastern[1])]
    side_c = [c_copy(0, 14, western[0]), c_copy(1, 15, eastern[0])]
    bulk = far_u[:2] + [far_h] + far_u[2:]

    loads[0].wait()
    loads[1].wait()
    for n in range(4):
        cut = slice(128 * n, 128 * n + 128)
        for k in range(STEPS):
            send_rows[0, n, PACK_ROWS[k] : PACK_ROWS[k] + 16] = hb[k, 0:16, cut].astype(jnp.float32)
        send_rows[0, n, 52:60] = cb[0:8, cut]
        for k in reversed(range(STEPS)):
            first = PACK_ROWS[k] - 2 * k
            send_rows[1, n, first : first + 16] = hb[k, 48:64, cut].astype(jnp.float32)
        send_rows[1, n, 52:60] = cb[56:64, cut]

    loads[2].wait()
    lane = lanes(ROWS)
    for side in (0, 1):
        packed = None
        for f, (w, o) in enumerate(zip(WIDTHS, LANES)):
            cut = slice(0, 128) if side == 0 else slice(COLS - 128, COLS)
            if f < 4:
                x = ub[f, :, cut]
            elif f < 8:
                x = hb[f - 4, :, cut].astype(jnp.float32)
            else:
                x = cb[:, cut]
            x = left(x, o if side == 0 else o + w)
            packed = x if packed is None else jnp.where(lane < o, packed, x)
        send_cols[side] = packed

    pl.semaphore_wait(barrier, 5 + jnp.where(first_row, 0, jnp.where(last_row, 3, 1)) - jnp.where(asks_west, 2, 0))

    @pl.when(last_row)
    def _():
        for d in [far] + corners:
            signal(answer.at[0], d)
        for c in direct_k:
            c.start()

    for d, special in zip(eastern, answers):

        @pl.when(special)
        def _():
            signal(answer.at[1], d)

    for c in near_u + [near_h, side_c[1], near_k[1]]:
        c.start()

    @pl.when(jnp.logical_not(asks_west))
    def _():
        for c in [side_c[0], near_k[0]]:
            c.start()

    @pl.when(jnp.logical_not(first_row))
    def _():
        for c in bulk:
            c.start()

    def inner_tiles(store, nat, rows):
        lane = lanes(rows)
        for j, shift in ((1, 40), (2, 64), (3, 88)):
            store(j, jnp.where(lane < shift, left(nat[j - 1], shift), left(nat[j], shift)))

    def outer_tiles(store, first, last, before, after, f, rows):
        lane = lanes(rows)
        w, o = WIDTHS[f], LANES[f]
        store(0, jnp.where(lane < 16, left(before, 16 - w - o), left(first, 16)))
        store(4, jnp.where(lane < 112, left(last, 112), left(after, 112 - o)))

    def put(f, start, rows):
        ref, lead = (U0, (f,)) if f < 4 else (H, (f - 4,)) if f < 8 else (PP, (4,))

        def store(j, value):
            ref[(*lead, j, pl.ds(start, rows))] = value

        return store

    def own(f, n):
        cut = slice(128 * n, 128 * n + 128)
        return ub[f, :, cut] if f < 4 else hb[f - 4, :, cut].astype(jnp.float32) if f < 8 else cb[:, cut]

    def lay_own(inner):
        for f in range(9):
            store = put(f, REACH, ROWS)
            if inner:
                inner_tiles(store, [own(f, n) for n in range(4)], ROWS)
            else:
                mine = slice(REACH, REACH + ROWS)
                outer_tiles(store, own(f, 0), own(f, 3), cols[0, mine], cols[1, mine], f, ROWS)

    def lay_halo(halo, fields, inner, outer):
        start = halo_start(halo)
        for f in fields:

            def part(n):
                if f < 4:
                    return rows_u[halo, f, :, 128 * n : 128 * n + 128]
                k = f - 4
                return rows_h[halo, n, pl.ds(PACK_ROWS[k] - (1 - halo) * (2 * k), REACH)]

            store = put(f, start, REACH)
            if inner:
                inner_tiles(store, [part(n) for n in range(4)], REACH)
            if outer:
                sides = [cols[side, pl.ds(start, REACH)] for side in (0, 1)]
                outer_tiles(store, part(0), part(3), *sides, f, REACH)

    def dot(x, w):
        return jnp.dot(x, w, preferred_element_type=jnp.float32)

    def halves(x):
        high = x.astype(jnp.bfloat16)
        return [high, (x - high.astype(jnp.float32)).astype(jnp.bfloat16)]

    def along(columns, kind):
        rows = columns[0][0].shape[0]
        if rows == REACH:
            return [along_rolled(xs, kind) for xs in columns]
        w = {"both": W[...], "slope": W[:, 0:128], "minus": WK[256:512], "step": WK[...]}[kind]
        stacked = [jnp.concatenate(sum([halves(x) for x in xs], []), axis=1) for xs in columns]
        out = dot(jnp.concatenate(stacked, axis=0), w)
        return [out[i * rows : i * rows + rows] for i in range(len(columns))]

    def along_rolled(xs, kind):
        x = xs[0]
        if kind == "step":
            my, two = xs[1], x + x
            ring = left(two + my, 1) + left(two - my, -1)
            return 8.0 * ring - (left(x + my, 2) + left(x - my, -2))
        w1, e1, w2, e2 = left(x, 1), left(x, -1), left(x, 2), left(x, -2)
        if kind == "minus":
            return 8.0 * (w1 - e1) - (w2 - e2)
        slope = 8.0 * (e1 - w1) - (e2 - w2)
        if kind == "slope":
            return slope
        return jnp.concatenate([slope, 16.0 * (e1 + w1) - (e2 + w2)], axis=1)

    def slopes(region, tiles):
        for k in range(STEPS):
            start, rows = region(2 * k + 2)
            here = pl.ds(start, rows)
            whole = jnp.concatenate([H[k, j, here].astype(jnp.bfloat16) for j in tiles], axis=0)
            cross = dot(whole, W[0:128, 0:128])
            for i, j in enumerate(tiles):
                at = lambda d: H[k, j, pl.ds(start + d, rows)]
                AR[k, j, here] = SLOPE * (8.0 * (at(1) - at(-1)) - (at(2) - at(-2)))
                AC[k, j, here] = SLOPE * cross[i * rows : i * rows + rows]

    def over(probes_of, tiles, batch, body):
        pairs = [(p, j) for p in probes_of for j in tiles]
        for i in range(0, len(pairs), batch):
            body(pairs[i : i + batch])

    def tangent(k, source, target, region):
        start, rows = region
        here = pl.ds(start, rows)

        def body(pairs):
            cross = along([[source[p, j, here]] for p, j in pairs], "slope" if target is None else "both")
            for (p, j), c in zip(pairs, cross):
                at = lambda d: source[p, j, pl.ds(start + d, rows)]
                n1, s1, n2, s2 = at(-1), at(1), at(-2), at(2)
                br = 8.0 * (s1 - n1) - (s2 - n2)
                bc = c[:, 0:128]
                if target is None:
                    M3[p, j, here] = PS[STEPS, j, here] * br
                    N3[p, j, here] = PS[STEPS, j, here] * bc
                    continue
                BR[k, p, j, here] = br
                BC[k, p, j, here] = bc
                lap = (16.0 * (n1 + s1) - (n2 + s2)) + c[:, 128:256]
                target[p, j, here] = KEEP * at(0) + A * (
                    lap + AR[k, j, here] * br + AC[k, j, here] * bc
                )

        return body

    def spread(q_at, m_at, cross):
        s = q_at(-1) + q_at(1)
        ring = (s + s) + (m_at(-1) - m_at(1))
        outer = (q_at(-2) + q_at(2)) + (m_at(-2) - m_at(2))
        return KEEP * q_at(0) + A * ((8.0 * ring - outer) + cross)

    def p_flux(region, tiles):
        start, rows = region
        here = pl.ds(start, rows)
        for j in tiles:
            x = PP[STEPS, j, here]
            PS[STEPS, j, here] = SLOPE * x
            MP[STEPS, j, here] = x * AR[STEPS - 1, j, here]

    def p_step(k, region, tiles):
        start, rows = region
        here = pl.ds(start, rows)
        cross = along([[PP[k + 1, j, here], PP[k + 1, j, here] * AC[k, j, here]] for j in tiles], "step")
        results = []
        for j, c in zip(tiles, cross):
            q_at = lambda d: PP[k + 1, j, pl.ds(start + d, rows)]
            m_at = lambda d: MP[k + 1, j, pl.ds(start + d, rows)]
            out = spread(q_at, m_at, c)
            if k > 0:
                PP[k, j, here] = out
                PS[k, j, here] = SLOPE * out
                MP[k, j, here] = out * AR[k - 1, j, here]
            results.append(out)
        if k == 0:
            to_natural(p_out, (), results, start, rows)

    def to_natural(ref, lead, tiles, start, rows):
        lane = lanes(rows)
        moved = [left(t, s) for t, s in zip(tiles, (112, 88, 64, 40, 16))]
        first = aligned(start - REACH)
        for n, edge in enumerate((100, 76, 52, 28)):
            ref[(*lead, pl.ds(first, rows), slice(128 * n, 128 * n + 128))] = jnp.where(
                lane < edge, moved[n], moved[n + 1]
            )

    def q_first(region):
        start, rows = region
        here = pl.ds(start, rows)

        def body(pairs):
            cross = along([[N3[p, j, here]] for p, j in pairs], "minus")
            for (p, j), c in zip(pairs, cross):
                m_at = lambda d: M3[p, j, pl.ds(start + d, rows)]
                out = A * ((8.0 * (m_at(-1) - m_at(1)) - (m_at(-2) - m_at(2))) + c)
                Q3[p, j, here] = out
                M2[p, j, here] = out * AR[2, j, here] + PS[3, j, here] * BR[2, p, j, here]

        return body

    def q_step(k, source, flux, target, next_flux, region):
        start, rows = region
        here = pl.ds(start, rows)

        def body(pairs):
            def operands(p, j):
                x = source[p, j, here]
                return [x, x * AC[k, j, here] + PS[k + 1, j, here] * BC[k, p, j, here]]

            cross = along([operands(p, j) for p, j in pairs], "step")
            results = []
            for (p, j), c in zip(pairs, cross):
                q_at = lambda d: source[p, j, pl.ds(start + d, rows)]
                m_at = lambda d: flux[p, j, pl.ds(start + d, rows)]
                out = spread(q_at, m_at, c)
                if target is not None:
                    target[p, j, here] = out
                if next_flux is not None:
                    next_flux[p, j, here] = out * AR[k - 1, j, here] + PS[k, j, here] * BR[k - 1, p, j, here]
                results.append(out)
            if target is None:
                for i in range(0, len(pairs), TILES):
                    to_natural(q_out, (pairs[i][0],), results[i : i + TILES], start, rows)

        return body

    def refresh(region):
        start, rows = region

        def body(pairs):
            here = pl.ds(start, rows)
            lane = lanes(rows)
            for p, j in pairs:
                x = Q2[p, j, here]
                if j > 0:
                    x = jnp.where(lane < 12, left(Q2[p, j - 1, here], -104), x)
                if j < TILES - 1:
                    x = jnp.where(lane >= 116, left(Q2[p, j + 1, here], 104), x)
                QR[p, j, here] = x
                M1[p, j, here] = x * AR[1, j, here] + PS[2, j, here] * BR[1, p, j, here]

        return body

    everyone, all_tiles = tuple(range(PROBES)), range(TILES)

    def shared(region, tiles):
        slopes(region, tiles)
        p_flux(region(8), tiles)

    def sweep(region, tiles, batch, which=everyone):
        run = functools.partial(over, which, tiles, batch)
        run(tangent(0, U0, U1, region(2)))
        p_step(3, region(10), tiles)
        run(tangent(1, U1, U2, region(4)))
        p_step(2, region(12), tiles)
        run(tangent(2, U2, U3, region(6)))
        p_step(1, region(14), tiles)
        run(tangent(3, U3, None, region(8)))
        run(q_first(region(10)))
        run(q_step(2, Q3, M2, Q2, None, region(12)))

    def finish(region, batch, which=everyone):
        run = functools.partial(over, which, all_tiles, batch)
        run(refresh(region(12)))
        p_step(0, region(16), all_tiles)
        run(q_step(1, QR, M1, Q1, M0, region(14)))
        run(q_step(0, Q1, M0, None, None, region(16)))

    lay_own(True)

    @pl.when(asks_west)
    def _():
        pl.semaphore_wait(answer.at[1], 2)
        for c in [side_c[0], near_k[0]]:
            c.start()

    def phases(core):
        near_halo, far_halo = 1 - core, core

        def main_region(margin):
            rows = (80 - 2 * margin + 15) // 16 * 16
            if margin == 16:
                return aligned(32 - 16 * core), rows
            return (1 - core) * (SPAN - margin - rows) + core * margin, rows

        for c in near_u + [near_h]:
            c.wait_recv()
        lay_halo(near_halo, range(9), True, False)
        shared(main_region, (1, 2, 3))
        sweep(main_region, (1, 2, 3), 6)

        @pl.when(first_row)
        def _():
            pl.semaphore_wait(answer.at[0], 3)
            for c in direct_k + bulk:
                c.start()

        for c in side_c:
            c.wait_recv()

        @pl.when(jnp.logical_not(first_row | last_row))
        def _():
            for c in far_k:
                c.start()

        lay_own(False)
        for c in near_k:
            c.wait_recv()
        lay_halo(near_halo, range(9), False, True)
        shared(main_region, (0, 4))
        sweep(main_region, (0, 4), 4)
        finish(main_region, 5)

        def wedge_region(margin):
            if margin == 16:
                return aligned(16 + 48 * core), REACH
            return (1 - core) * margin + core * (80 - margin), REACH

        for c in [far_h] + far_u + far_k:
            c.wait_recv()
        lay_halo(far_halo, range(9), True, True)
        shared(wedge_region, all_tiles)
        sweep(wedge_region, all_tiles, 5)
        finish(wedge_region, 5)

    @pl.when(core == 0)
    def _():
        phases(0)

    @pl.when(core == 1)
    def _():
        phases(1)

    for c in far_u + [far_h] + far_k + near_u + [near_h] + near_k + side_c:
        c.wait_send()


def store_all(q, p, q_out, p_out, sem):
    copies = [
        pltpu.make_async_copy(q, q_out, sem.at[0]),
        pltpu.make_async_copy(p, p_out, sem.at[1]),
    ]
    for c in copies:
        c.start()
    for c in copies:
        c.wait()


def on_device(heights, probes, cotangent):
    f32 = jnp.float32
    probe = pltpu.VMEM((PROBES, TILES, SPAN, 128), f32)
    steps = pltpu.VMEM((STEPS + 1, TILES, SPAN, 128), f32)
    slope = pltpu.VMEM((3, PROBES, TILES, SPAN, 128), f32)
    q, p = pl.pallas_call(
        kernel,
        out_shape=[pltpu.VMEM((PROBES, ROWS, COLS), f32), pltpu.VMEM((ROWS, COLS), f32)],
        in_specs=[pl.BlockSpec(memory_space=pl.ANY)] * 3,
        out_specs=[pl.BlockSpec(memory_space=pltpu.VMEM)] * 2,
        scratch_shapes=[
            pltpu.VMEM((STEPS, ROWS, COLS), jnp.bfloat16),
            pltpu.VMEM((PROBES, ROWS, COLS), f32),
            pltpu.VMEM((ROWS, COLS), f32),
            pltpu.VMEM((2, 4, 72, 128), f32),
            pltpu.VMEM((2, PROBES, REACH, COLS), f32),
            pltpu.VMEM((2, 4, 72, 128), f32),
            pltpu.VMEM((2, ROWS, 128), f32),
            pltpu.VMEM((2, SPAN, 128), f32),
            probe,
            probe, probe, probe, probe,
            probe, probe,
            slope, slope,
            steps, steps, steps,
            probe, probe, probe, probe, probe, probe, probe, probe, probe,
            pltpu.VMEM((256, 256), jnp.bfloat16),
            pltpu.VMEM((512, 128), jnp.bfloat16),
            pltpu.SemaphoreType.DMA((3,)),
            pltpu.SemaphoreType.DMA((16,)),
            pltpu.SemaphoreType.DMA((16,)),
            pltpu.SemaphoreType.REGULAR((2,)),
        ],
        compiler_params=pltpu.CompilerParams(
            collective_id=0, has_side_effects=True, vmem_limit_bytes=56 * 2**20
        ),
    )(heights, probes, cotangent)
    return pl.pallas_call(
        store_all,
        out_shape=[jax.ShapeDtypeStruct(q.shape, f32), jax.ShapeDtypeStruct(p.shape, f32)],
        in_specs=[pl.BlockSpec(memory_space=pltpu.VMEM)] * 2,
        out_specs=[pl.BlockSpec(memory_space=pl.ANY)] * 2,
        scratch_shapes=[pltpu.SemaphoreType.DMA((2,))],
    )(
        pltpu.with_memory_space_constraint(q, pltpu.VMEM),
        pltpu.with_memory_space_constraint(p, pltpu.VMEM),
    )


def solution(mesh):
    in_specs = (P(None, "gx", "gy"), P(None, "gx", "gy"), P("gx", "gy"))
    out_specs = (P(None, "gx", "gy"), P("gx", "gy"))
    return jax.shard_map(
        on_device, mesh=mesh, in_specs=in_specs, out_specs=out_specs, check_vma=False
    )
```
